32 devices in a mesh: grp: 2 (over x), scen: 8 (over z, y), bund: 2 (over core).
Axes of the slice: x: 2, y: 2, z: 4, core: 2. Of those that a mesh axis runs over, the one named last changes fastest.
Arguments:
- constraint: bfloat16 [2048, 2, 64, 128], P(('grp', 'scen', 'bund')), parts along dimension 0, may hold values from -0.5 to 0.5
- demand: bfloat16 [2048, 2, 64], P(('grp', 'scen', 'bund')), parts along dimension 0, may hold values from -6 to 6
- start_duals: bfloat16 [2048, 2, 64], P(('grp', 'scen', 'bund')), parts along dimension 0, may hold values from -4 to 4
- unit_cost: bfloat16 [2048, 2, 128], P(('grp', 'scen', 'bund')), parts along dimension 0, may hold values from -4 to 4
- multiplier: bfloat16 [2048, 2, 128], P(('grp', 'scen', 'bund')), parts along dimension 0, may hold values from -4 to 4
- weight: bfloat16 [2048], P(('grp', 'scen', 'bund')), parts along dimension 0, may hold values from 0.25 to 4
- block_index: int32 [2048, 2], P(('grp', 'scen', 'bund')), parts along dimension 0, may hold values from 0 to 1023
- bundle_of: int32 [2048], P(('grp', 'scen', 'bund')), parts along dimension 0, may hold values from 0 to 15, as said below
- consensus: float32 [2097152], P(('grp', 'scen', 'bund')), parts along dimension 0, may hold values from 0 to 1
- capacity_limit: float32 [2097152], P(('grp', 'scen', 'bund')), parts along dimension 0, may hold values from 0.6 to 1.5
Outputs:
- consensus_new: float32 [2097152], P(('grp', 'scen', 'bund')), parts along dimension 0
- multiplier_new: float32 [2048, 2, 128], P(('grp', 'scen', 'bund')), parts along dimension 0
The draws below stay inside these ranges and needn't reach their ends.
There are 2 independent parts, one for each index of `grp`. The reference program is written for one: setup_inputs(seed, part) draws one part's arguments, and reference() takes and returns one part's arrays. A program takes and returns all parts, laid end to end along the dimension named above; each array names one. Nothing has to cross between parts.
Inputs may be any that keep to these rules, and one draw needn't show every extreme that they name: `bundle_of`: at most 8 of the 64 scenarios of one device belong to one bundle; one bundle gets exactly 8 scenarios from every device.
All inputs are finite; a program needn't handle non-finite values.
Results may differ from the reference program's by a relative error of at most 0.0003.
Values may be sent and summed in bfloat16 or wider, within the bound.
A program may use at most 128 MiB of HBM per device.

```python
import math
import jax
import jax.numpy as jnp
from jax import lax

NCAP = 1048576
CB = 128
RB = 64
KB = 2
SC_DEV = 64
NBUN = 16
SCEN = 1024
C = 8
NBLK = 8192
SB = 512


def draw_bundle_of(key, part):
    key = jax.random.fold_in(key, 7)
    busiest_key, device_keys = jax.random.split(key)
    busiest = jax.random.randint(busiest_key, (), 0, NBUN)
    candidates = jnp.arange(NBUN * C, dtype=jnp.int32) // C

    def one_device(device_key):
        first_key, second_key = jax.random.split(device_key)
        shuffled = candidates[jax.random.permutation(first_key, NBUN * C)]
        ordering = jnp.argsort((shuffled != busiest).astype(jnp.int32), stable=True)
        chosen = shuffled[ordering][:SC_DEV]
        return chosen[jax.random.permutation(second_key, SC_DEV)]
    return jax.vmap(one_device)(jax.random.split(device_keys, NBUN)).reshape(-1).astype(jnp.int32)


def plant(array, rng, least, top_value):
    spot = [jax.random.randint(jax.random.fold_in(rng, axis), (), 0, length) for axis, length in enumerate(array.shape)]
    widest = array.shape.index(max(array.shape))
    neighbour = spot[:widest] + [(spot[widest] + 1) % array.shape[widest]] + spot[widest + 1:]
    return array.at[tuple(spot)].set(least).at[tuple(neighbour)].set(top_value)


def shard_levels(own_key, shape, shards, smallest, top_value):
    loudness = 1.0
    for axis_at, parts in shards:
        draws = jax.random.uniform(jax.random.fold_in(jax.random.fold_in(own_key, 6), axis_at), (parts,), jnp.float32, smallest / len(shards), top_value / len(shards))
        loudness = loudness * jnp.repeat(jnp.exp(draws), shape[axis_at] // parts).reshape((-1,) + (1,) * (len(shape) - 1 - axis_at))
    return loudness


def centred(own_key, extent, spread, reach, pieces=(), held_as=jnp.bfloat16):
    loudness = shard_levels(own_key, extent, pieces, -0.22, 0.18) if pieces else 1.0
    values = jax.random.normal(own_key, extent, jnp.float32) * spread * loudness
    return jnp.minimum(jnp.maximum(values, -reach), reach).astype(held_as)


def setup_inputs(seed: int = 0, part: int = 0) -> dict:
    seeds = jax.random.split(jax.random.key(seed), 11)
    part_splits = jax.random.split(jax.random.fold_in(seeds[10], part), 11)
    return {
        "constraint": centred(part_splits[0], (SCEN, KB, RB, CB), CB ** -0.5, 0.5, ((0, 16),)),
        "demand": centred(part_splits[1], (SCEN, KB, RB), 1.0, 6.0, ((0, 16),)),
        "start_duals": centred(part_splits[2], (SCEN, KB, RB), 0.5, 4.0, ((0, 16),)),
        "unit_cost": centred(part_splits[3], (SCEN, KB, CB), 0.5, 4.0, ((0, 16),)),
        "multiplier": centred(part_splits[4], (SCEN, KB, CB), 0.5, 4.0, ((0, 16),)),
        "weight": jnp.clip(jnp.exp(math.log(4.0) - 2.7725887 * jax.random.uniform(part_splits[5], (SCEN,), jnp.float32) ** shard_levels(part_splits[5], (SCEN,), ((0, 16),), -0.2, 0.2)), 0.25, 4.0).astype(jnp.bfloat16),
        "block_index": plant(jax.random.randint(part_splits[6], (SCEN, KB), 0, 2 * SB), jax.random.fold_in(part_splits[6], 1), 0, (2 * SB) - 1).astype(jnp.int32),
        "bundle_of": draw_bundle_of(jax.random.fold_in(jax.random.fold_in(seeds[10], part), 71), part),
        "consensus": jnp.clip(1.0 * jax.random.uniform(part_splits[8], (NCAP,), jnp.float32) ** shard_levels(part_splits[8], (NCAP,), ((0, 16),), -0.2, 0.2), 0.0, 1.0),
        "capacity_limit": jnp.clip(0.6 + 0.9 * jax.random.uniform(part_splits[9], (NCAP,), jnp.float32) ** shard_levels(part_splits[9], (NCAP,), ((0, 16),), -0.2, 0.2), 0.6, 1.5),
    }


penalty = 1.0
dual_step = 0.5
step_size = 0.5
anchor = 1.0


def exact_einsum(pattern, left_side, right_side):
    return jnp.einsum(pattern, left_side, right_side, precision=lax.Precision.HIGHEST, preferred_element_type=jnp.float32)


def reference(constraint, demand, start_duals, unit_cost, multiplier, weight, block_index, bundle_of, consensus, capacity_limit):
    region_len = 2 * SB
    segments = NBUN * region_len
    matrices = constraint.astype(jnp.float32)
    targets = demand.astype(jnp.float32)
    duals_zero = start_duals.astype(jnp.float32)
    mult_old = multiplier.astype(jnp.float32)
    linear_terms = unit_cost.astype(jnp.float32) + mult_old
    weights = weight.astype(jnp.float32)
    flat_ids = (bundle_of.astype(jnp.int32)[:, None] * region_len + block_index.astype(jnp.int32)).reshape(-1)
    pair_weight = jnp.broadcast_to(weights[:, None], (SCEN, KB)).reshape(-1)
    totals = jax.ops.segment_sum(pair_weight, flat_ids, num_segments=segments)
    offsets = jnp.arange(region_len, dtype=jnp.int32)
    global_blocks = ((jnp.arange(NBUN, dtype=jnp.int32)[:, None] * SB + offsets[None, :]) % NBLK).reshape(-1)
    old_blocks = consensus.reshape(NBLK, CB)
    limit_blocks = capacity_limit.reshape(NBLK, CB)
    region_old = old_blocks[global_blocks]
    region_high = limit_blocks[global_blocks]

    def pick_rows(region):
        return region[flat_ids].reshape(SCEN, KB, CB)

    prior = pick_rows(region_old)

    def residual_of(current):
        return exact_einsum("skrc,skc->skr", matrices, pick_rows(current)) - targets

    def descend(current, inner_duals):
        local_cols = pick_rows(current)
        pulled = exact_einsum("skrc,skr->skc", matrices, inner_duals)
        slot_terms = weights[:, None, None] * (linear_terms + pulled + penalty * (local_cols - prior))
        gradient = jax.ops.segment_sum(slot_terms.reshape(-1, CB), flat_ids, num_segments=segments)
        return jnp.clip(current - step_size * gradient / (1.0 + totals)[:, None], 0.0, region_high)

    first_res = residual_of(region_old)
    zone_one = descend(region_old, duals_zero + dual_step * first_res)
    second_res = residual_of(zone_one)
    duals_next = duals_zero + dual_step * second_res
    zone_two = descend(zone_one, duals_next + dual_step * second_res)
    weighted = totals[:, None] * zone_two
    numer = anchor * old_blocks + jax.ops.segment_sum(weighted, global_blocks, num_segments=NBLK)
    denom = anchor + jax.ops.segment_sum(totals, global_blocks, num_segments=NBLK)
    fresh = numer / denom[:, None]
    scen_blocks = global_blocks[flat_ids]
    fresh_cols = fresh[scen_blocks].reshape(SCEN, KB, CB)
    multiplier_new = mult_old + penalty * (pick_rows(zone_two) - fresh_cols)
    return fresh.reshape(NCAP), multiplier_new
```

```python
import functools
import jax
import jax.numpy as jnp
from jax import lax
from jax.experimental import pallas as pl
from jax.experimental.pallas import tpu as pltpu
from jax.sharding import PartitionSpec as P

f32 = jnp.float32
bf16 = jnp.bfloat16
i32 = jnp.int32
CHUNK = 16


def split(x):
    hi = x.astype(bf16)
    lo = (x - hi.astype(f32)).astype(bf16)
    return jnp.concatenate([hi, lo], axis=1)


def mm(a, b):
    return jnp.dot(a, b, preferred_element_type=f32)


def mm_split(sel, x):
    out = mm(sel, split(x))
    c = x.shape[1]
    return out[:, :c] + out[:, c:]


def onehot(cond):
    return jnp.where(cond, 1.0, 0.0).astype(bf16)


def to_bytes(q):
    hi = lax.shift_right_logical(q, 8)
    lo = q & 255
    return jnp.concatenate([hi.astype(f32).astype(bf16), lo.astype(f32).astype(bf16)], axis=1)


def pack(q):
    half = q.shape[0] // 2
    return (q[:half] << 16) | q[half:]


def unpack(word):
    return jnp.concatenate([lax.shift_right_logical(word, 16), word & 65535], axis=0)


def kernel(
    n, n_bund, rh, sb, rb,
    meta_ref, lin_ref, base1_ref, base2_ref, a_ref, old_ref, high_ref,
    fresh_ref, diff_ref,
    meta_out, meta_in, rows_out, rows_in, scale_out, scale_in,
    e_ref, eq_ref, g_ref, gt_ref,
    send_sem, recv_sem, scale_send, scale_recv,
):
    me = lax.axis_index("scen") * n_bund + lax.axis_index("bund")
    pairs = meta_ref.shape[1]
    cols = old_ref.shape[1]
    half_slots = n * rh
    slots = 2 * half_slots

    def device(e):
        d = lax.rem(me + 1 + e, n)
        return {"scen": d // n_bund, "bund": lax.rem(d, n_bund)}

    barrier = pltpu.get_barrier_semaphore()

    def greet(e, c):
        pl.semaphore_signal(barrier, inc=1, device_id=device(e), device_id_type=pl.DeviceIdType.MESH)
        return c

    lax.fori_loop(0, n - 1, greet, 0)

    meta = meta_ref[...]
    meta_t = jnp.concatenate([meta] * (pairs // 8), axis=0).T
    bun_row, key_row, w_row = meta[0:1], meta[1:2], meta[2:3]
    bun_col, key_col, w_col = meta_t[:, 0:1], meta_t[:, 1:2], meta_t[:, 2:3]
    p_row = lax.broadcasted_iota(i32, (1, pairs), 1)
    p_col = lax.broadcasted_iota(i32, (pairs, 1), 0)
    same = bun_col == bun_row
    before = (p_row // 2) < (p_col // 2)
    after = (p_col // 2) < (p_row // 2)
    cnt_col = jnp.sum(jnp.where(same & before, 1.0, 0.0), axis=1, keepdims=True).astype(i32)
    cnt_row = jnp.sum(jnp.where(same & after, 1.0, 0.0), axis=0, keepdims=True).astype(i32)

    def code(bun, key, cnt, p):
        up = (key.astype(i32) >= sb).astype(i32)
        dest = bun.astype(i32) + up
        dest = jnp.where(dest >= n, dest - n, dest)
        entry = dest - me - 1
        entry = jnp.where(entry < 0, entry + n, entry)
        inner = cnt + (p & 1)
        return dest * (2 * rh) + up * rh + inner, up * half_slots + entry * rh + inner

    full_row, rel_row = code(bun_row, key_row, cnt_row, p_row)
    _, rel_col = code(bun_col, key_col, cnt_col, p_col)
    meta_out[...] = jnp.concatenate(
        [full_row.astype(f32), key_row, w_row, jnp.zeros((5, pairs), f32)], axis=0
    )
    pl.semaphore_wait(barrier, n - 1)

    def exchange_start(src_of, dst, ssem, rsem):
        def go(e, c):
            pltpu.make_async_remote_copy(
                src_ref=src_of(e), dst_ref=dst.at[n - 2 - e], send_sem=ssem, recv_sem=rsem,
                device_id=device(e), device_id_type=pl.DeviceIdType.MESH,
            ).start()
            return c
        lax.fori_loop(0, n - 1, go, 0)

    def wait_all(buf, sem):
        part = buf.at[pl.ds(0, n - 1)]
        pltpu.make_async_copy(part, part, sem).wait()

    exchange_start(lambda e: meta_out, meta_in, send_sem.at[0], recv_sem.at[0])
    meta_in[n - 1] = meta_out[...]
    g_ref[...] = onehot(rel_col == lax.broadcasted_iota(i32, (pairs, slots), 1))
    gt_ref[...] = onehot(rel_row == lax.broadcasted_iota(i32, (slots, pairs), 0))
    wait_all(meta_in, recv_sem.at[0])

    got = meta_in[...]
    code_in, key_in, w_in = got[:, 0:1, :], got[:, 1:2, :], got[:, 2:3, :]

    def slot_mask(h):
        want = me * (2 * rh) + h * rh + lax.broadcasted_iota(i32, (n, rh, pairs), 1)
        return code_in.astype(i32) == want

    masks = [slot_mask(0), slot_mask(1)]

    def slot_col(values):
        return jnp.concatenate(
            [
                jnp.sum(jnp.where(m, values, 0.0), axis=2, keepdims=True).reshape(half_slots, 1)
                for m in masks
            ],
            axis=0,
        )

    keys = slot_col(key_in + 1.0)
    w_slot = slot_col(w_in)
    up_slot = lax.broadcasted_iota(i32, (slots, 1), 0) >= half_slots
    local = jnp.where(up_slot, keys - sb, keys)
    local = jnp.where(keys > 0.0, local, 0.0)
    keys_row = jnp.broadcast_to(keys, (slots, 128)).T[0:1]
    local_row = jnp.broadcast_to(local, (slots, 128)).T[0:1]
    e_ref[...] = onehot(keys == keys_row)
    eq_ref[...] = onehot(local == local_row)
    own = onehot(local == lax.broadcasted_iota(i32, (slots, sb), 1).astype(f32) + 1.0)

    def send_rows(stage, codes):
        rows_out[stage] = pack(codes).reshape(n, rh, cols)
        exchange_start(
            lambda e: rows_out.at[stage, e], rows_in.at[stage], send_sem.at[stage + 1], recv_sem.at[stage + 1]
        )
        rows_in[stage, n - 1] = rows_out[stage, n - 1]

    def take_rows(stage):
        wait_all(rows_in.at[stage], recv_sem.at[stage + 1])
        return unpack(rows_in[stage].reshape(half_slots, cols))

    def zone_code(z):
        return jnp.minimum(jnp.round(z * 32768.0), 65535.0).astype(i32)

    prior = mm_split(own, old_ref[...])
    send_rows(0, zone_code(prior))
    high = mm_split(own, high_ref[...])
    w_wide = jnp.broadcast_to(w_slot, (slots, cols)).astype(bf16)
    totals = mm(e_ref[...], w_wide)
    step = 0.5 / (1.0 + totals)

    def home(stage, which, base_ref, dual):
        x = mm(g_ref[...], to_bytes(take_rows(stage))).astype(bf16)
        lanes = CHUNK * rb
        diag = lax.broadcasted_iota(i32, (CHUNK, lanes), 0) == (
            lax.broadcasted_iota(i32, (CHUNK, lanes), 1) // rb
        )
        pulled = []
        for c in range(pairs // CHUNK):
            a = a_ref[c * lanes:(c + 1) * lanes, :]
            xc = x[c * CHUNK:(c + 1) * CHUNK]
            xc = jnp.concatenate([xc[:, :cols], xc[:, cols:]], axis=0)
            r = lax.dot_general(xc, a, (((1,), (1,)), ((), ())), preferred_element_type=f32)
            r = (r[:CHUNK] * 256.0 + r[CHUNK:]) * (dual / 32768.0)
            inner = jnp.where(diag, r + base_ref[c:c + 1, :], 0.0)
            hi = inner.astype(bf16)
            lo = (inner - hi.astype(f32)).astype(bf16)
            g = mm(jnp.concatenate([hi, lo], axis=0), a)
            pulled.append(g[:CHUNK] + g[CHUNK:])
        terms = w_col * (lin_ref[...] + jnp.concatenate(pulled, axis=0))
        peak = jnp.maximum(jnp.max(jnp.abs(terms), axis=1, keepdims=True), 1e-30)
        unit = peak * (1.0 / 32767.0)
        scale_out[which] = jnp.broadcast_to(unit, (pairs, 128)).T[0:8]
        codes = jnp.round(terms / unit) + 32768.0
        codes = jnp.clip(codes, 0.0, 65535.0).astype(i32)
        exchange_start(lambda e: scale_out.at[which], scale_in.at[which], scale_send.at[which], scale_recv.at[which])
        scale_in[which, n - 1] = scale_out[which]
        placed = mm(gt_ref[...], to_bytes(codes))
        placed = (placed[:, :cols] * 256.0 + placed[:, cols:]).astype(i32)
        send_rows(stage + 1, placed)

    def gradient(stage, which):
        wait_all(scale_in.at[which], scale_recv.at[which])
        unit = slot_col(scale_in[which][:, 0:1, :])
        codes = take_rows(stage)
        terms = (codes - 32768).astype(f32) * unit
        return mm_split(e_ref[...], terms)

    home(0, 0, base1_ref, 0.5)
    zone_one = jnp.clip(prior - step * gradient(1, 0), 0.0, high)
    send_rows(2, zone_code(zone_one))
    home(2, 1, base2_ref, 1.0)
    grad = gradient(3, 1) + totals * (zone_one - prior)
    zone_two = jnp.clip(zone_one - step * grad, 0.0, high)
    weighted = w_slot * zone_two
    both = jnp.concatenate([split(weighted), w_wide], axis=1)
    sums = mm(eq_ref[...], both)
    fresh = (prior + (sums[:, :cols] + sums[:, cols:2 * cols])) / (1.0 + sums[:, 2 * cols:])
    delta = jnp.round((zone_two - fresh + 2.0) * 16384.0)
    send_rows(4, jnp.clip(delta, 0.0, 65535.0).astype(i32))
    own_t = onehot(local_row == lax.broadcasted_iota(i32, (sb, slots), 0).astype(f32) + 1.0)
    sums = mm(own_t, both)
    fresh_ref[...] = (old_ref[...] + (sums[:, :cols] + sums[:, cols:2 * cols])) / (
        1.0 + sums[:, 2 * cols:]
    )
    out = mm(g_ref[...], to_bytes(take_rows(4)))
    diff_ref[...] = (out[:, :cols] * 256.0 + out[:, cols:]) * (1.0 / 16384.0) - 2.0

    wait_all(meta_in, send_sem.at[0])
    for stage in range(5):
        wait_all(rows_in.at[stage], send_sem.at[stage + 1])
    for which in range(2):
        wait_all(scale_in.at[which], scale_send.at[which])


def body(
    constraint, demand, start_duals, unit_cost, multiplier, weight,
    block_index, bundle_of, consensus, capacity_limit,
):
    n = lax.axis_size(("scen", "bund"))
    n_bund = lax.axis_size("bund")
    per_dev, touched, rb, cols = constraint.shape
    pairs = per_dev * touched
    sb = consensus.shape[0] // cols
    capacity = max(2, (2 * per_dev + n - 1) // n)
    rh = -(-capacity * touched // 8) * 8
    half_slots = n * rh
    slots = 2 * half_slots

    wide = lambda v: jnp.broadcast_to(v.astype(f32)[:, None], (per_dev, touched)).reshape(1, pairs)
    meta = jnp.concatenate(
        [wide(bundle_of), block_index.astype(f32).reshape(1, pairs), wide(weight), jnp.zeros((5, pairs), f32)],
        axis=0,
    )
    mult = multiplier.astype(f32)
    lin = (unit_cost.astype(f32) + mult).reshape(pairs, cols)
    duals = start_duals.astype(f32)
    target = demand.astype(f32)
    lanes = CHUNK * rb
    base1 = (duals - 0.5 * target).reshape(pairs * rb // lanes, lanes)
    base2 = (duals - target).reshape(pairs * rb // lanes, lanes)

    vmem = pl.BlockSpec(memory_space=pltpu.VMEM)
    fresh, diff = pl.pallas_call(
        functools.partial(kernel, n, n_bund, rh, sb, rb),
        out_shape=(
            jax.ShapeDtypeStruct((sb, cols), f32),
            jax.ShapeDtypeStruct((pairs, cols), f32),
        ),
        in_specs=[vmem] * 7,
        out_specs=(vmem, vmem),
        scratch_shapes=[
            pltpu.VMEM((8, pairs), f32),
            pltpu.VMEM((n, 8, pairs), f32),
            pltpu.VMEM((5, n, rh, cols), i32),
            pltpu.VMEM((5, n, rh, cols), i32),
            pltpu.VMEM((2, 8, pairs), f32),
            pltpu.VMEM((2, n, 8, pairs), f32),
            pltpu.VMEM((slots, slots), bf16),
            pltpu.VMEM((slots, slots), bf16),
            pltpu.VMEM((pairs, slots), bf16),
            pltpu.VMEM((slots, pairs), bf16),
            pltpu.SemaphoreType.DMA((6,)),
            pltpu.SemaphoreType.DMA((6,)),
            pltpu.SemaphoreType.DMA((2,)),
            pltpu.SemaphoreType.DMA((2,)),
        ],
        compiler_params=pltpu.CompilerParams(
            collective_id=0, has_side_effects=True, vmem_limit_bytes=56 * 1024 * 1024
        ),
    )(
        meta, lin, base1, base2,
        constraint.reshape(pairs * rb, cols),
        consensus.reshape(sb, cols),
        capacity_limit.reshape(sb, cols),
    )
    return fresh.reshape(-1), mult + diff.reshape(per_dev, touched, cols)


def solution(mesh):
    split_all = ("grp", "scen", "bund")
    return jax.shard_map(
        body,
        mesh=mesh,
        in_specs=(
            P(split_all, None, None, None),
            P(split_all, None, None),
            P(split_all, None, None),
            P(split_all, None, None),
            P(split_all, None, None),
            P(split_all),
            P(split_all, None),
            P(split_all),
            P(split_all),
            P(split_all),
        ),
        out_specs=(P(split_all), P(split_all, None, None)),
        check_vma=False,
    )
```

```python
import functools
import jax
import jax.numpy as jnp
from jax import lax
from jax.experimental import pallas as pl
from jax.experimental.pallas import tpu as pltpu
from jax.sharding import PartitionSpec as P

f32 = jnp.float32
bf16 = jnp.bfloat16
i32 = jnp.int32
CHUNK = 16


def split(x):
    hi = x.astype(bf16)
    lo = (x - hi.astype(f32)).astype(bf16)
    return jnp.concatenate([hi, lo], axis=1)


def mm(a, b):
    return jnp.dot(a, b, preferred_element_type=f32)


def mm_split(sel, x):
    out = mm(sel, split(x))
    c = x.shape[1]
    return out[:, :c] + out[:, c:]


def onehot(cond):
    return jnp.where(cond, 1.0, 0.0).astype(bf16)


def to_bytes(q):
    hi = lax.shift_right_logical(q, 8)
    lo = q & 255
    return jnp.concatenate([hi.astype(f32).astype(bf16), lo.astype(f32).astype(bf16)], axis=1)


def pack(q):
    half = q.shape[0] // 2
    return (q[:half] << 16) | q[half:]


def unpack(word):
    return jnp.concatenate([lax.shift_right_logical(word, 16), word & 65535], axis=0)


def kernel(
    n, n_bund, rh, sb, rb,
    bundle_ref, block_ref, weight_ref, unit_ref, mult_ref, dual_ref, demand_ref, a_hbm, old_ref, high_ref,
    fresh_ref, out_ref,
    meta_out, meta_in, rows_out, rows_in, scale_out, scale_in,
    e_ref, eq_ref, g_ref, gt_ref, own_ref, own_t_ref, a_ref, lin_ref, base_ref,
    send_sem, recv_sem, scale_send, scale_recv, a_sem,
):
    me = lax.axis_index("scen") * n_bund + lax.axis_index("bund")
    per_dev, touched = block_ref.shape
    pairs = per_dev * touched
    cols = old_ref.shape[1]
    half_slots = n * rh
    slots = 2 * half_slots

    bits = n.bit_length() - 1
    mine = [lax.rem(me // (1 << b), 2) for b in range(bits)]

    def device(e):
        d = 0
        for b in range(bits):
            k = lax.rem((e + 1) // (1 << b), 2)
            d = d + (mine[b] + k - 2 * mine[b] * k) * (1 << b)
        return {"scen": d // n_bund, "bund": lax.rem(d, n_bund)}

    barrier = pltpu.get_barrier_semaphore()

    def greet(e, c):
        pl.semaphore_signal(barrier, inc=1, device_id=device(e), device_id_type=pl.DeviceIdType.MESH)
        return c

    lax.fori_loop(0, n - 1, greet, 0)

    load_a = pltpu.make_async_copy(a_hbm, a_ref, a_sem)
    load_a.start()

    twice = lambda row: jnp.concatenate([row] * touched, axis=1)
    bun_row = twice(bundle_ref[...].astype(f32))
    w_row = twice(weight_ref[...].astype(f32))
    key_col = jnp.concatenate([block_ref[:, j:j + 1] for j in range(touched)], axis=0).astype(f32)
    rows = jnp.concatenate([bun_row, w_row, jnp.zeros((6, pairs), f32)], axis=0)
    rows_t = jnp.concatenate([rows] * (pairs // 8), axis=0).T
    bun_col, w_col = rows_t[:, 0:1], rows_t[:, 1:2]
    key_row = jnp.broadcast_to(key_col, (pairs, 128)).T[0:1]
    p_row = lax.broadcasted_iota(i32, (1, pairs), 1)
    p_col = lax.broadcasted_iota(i32, (pairs, 1), 0)
    same = bun_col == bun_row
    before = (p_row < per_dev) & (p_row < lax.rem(p_col, per_dev))
    after = (p_col < per_dev) & (p_col < lax.rem(p_row, per_dev))
    cnt_col = jnp.sum(jnp.where(same & before, 1.0, 0.0), axis=1, keepdims=True).astype(i32)
    cnt_row = jnp.sum(jnp.where(same & after, 1.0, 0.0), axis=0, keepdims=True).astype(i32)

    def code(bun, key, cnt, p):
        up = (key.astype(i32) >= sb).astype(i32)
        dest = bun.astype(i32) + up
        dest = jnp.where(dest >= n, dest - n, dest)
        entry = jnp.where(dest == me, n, dest ^ me) - 1
        inner = cnt * touched + p // per_dev
        return dest * (2 * rh) + up * rh + inner, up * half_slots + entry * rh + inner

    full_row, rel_row = code(bun_row, key_row, cnt_row, p_row)
    _, rel_col = code(bun_col, key_col, cnt_col, p_col)
    meta_out[...] = jnp.concatenate([full_row.astype(f32), key_row, w_row], axis=1)
    pl.semaphore_wait(barrier, n - 1)

    def exchange_start(src_of, dst, ssem, rsem):
        def go(k, c):
            e = n - 2 - k
            pltpu.make_async_remote_copy(
                src_ref=src_of(e), dst_ref=dst.at[e], send_sem=ssem, recv_sem=rsem,
                device_id=device(e), device_id_type=pl.DeviceIdType.MESH,
            ).start()
            return c
        lax.fori_loop(0, n - 1, go, 0)

    def wait_all(buf, sem):
        part = buf.at[pl.ds(0, n - 1)]
        pltpu.make_async_copy(part, part, sem).wait()

    exchange_start(lambda e: meta_out, meta_in, send_sem.at[0], recv_sem.at[0])
    meta_in[n - 1] = meta_out[...]
    g_ref[...] = onehot(rel_col == lax.broadcasted_iota(i32, (pairs, slots), 1))
    gt_ref[...] = onehot(rel_row == lax.broadcasted_iota(i32, (slots, pairs), 0))
    wait_all(meta_in, recv_sem.at[0])

    got = meta_in[...]
    code_in, key_in, w_in = [got[:, :, i * pairs:(i + 1) * pairs] for i in range(3)]

    def slot_mask(h):
        want = me * (2 * rh) + h * rh + lax.broadcasted_iota(i32, (n, rh, pairs), 1)
        return code_in.astype(i32) == want

    masks = [slot_mask(0), slot_mask(1)]

    def slot_col(values):
        return jnp.concatenate(
            [
                jnp.sum(jnp.where(m, values, 0.0), axis=2, keepdims=True).reshape(half_slots, 1)
                for m in masks
            ],
            axis=0,
        )

    keys = slot_col(key_in + 1.0)
    w_slot = slot_col(w_in)
    up_slot = lax.broadcasted_iota(i32, (slots, 1), 0) >= half_slots
    local = jnp.where(up_slot, keys - sb, keys)
    local = jnp.where(keys > 0.0, local, 0.0)
    keys_row = jnp.broadcast_to(keys, (slots, 128)).T[0:1]
    local_row = jnp.broadcast_to(local, (slots, 128)).T[0:1]
    own_ref[...] = onehot(local == lax.broadcasted_iota(i32, (slots, sb), 1).astype(f32) + 1.0)

    def send_rows(stage, codes):
        rows_out[stage] = pack(codes).reshape(n, rh, cols)
        exchange_start(
            lambda e: rows_out.at[stage, e], rows_in.at[stage], send_sem.at[stage + 1], recv_sem.at[stage + 1]
        )
        rows_in[stage, n - 1] = rows_out[stage, n - 1]

    def take_rows(stage):
        wait_all(rows_in.at[stage], recv_sem.at[stage + 1])
        return unpack(rows_in[stage].reshape(half_slots, cols))

    def zone_code(z):
        return jnp.minimum(jnp.round(z * 32768.0), 65535.0).astype(i32)

    prior = mm_split(own_ref[...], old_ref[...])
    send_rows(0, zone_code(prior))
    high = mm_split(own_ref[...], high_ref[...])
    e_ref[...] = onehot(keys == keys_row)
    w_wide = jnp.broadcast_to(w_slot, (slots, cols)).astype(bf16)
    totals = mm(e_ref[...], w_wide)
    step = 0.5 / (1.0 + totals)

    for j in range(touched):
        at = slice(j * per_dev, (j + 1) * per_dev)
        lin_ref[at] = unit_ref[:, j, :].astype(f32) + mult_ref[:, j, :].astype(f32)
        base_ref[0, at] = dual_ref[:, j, :].astype(f32)
        base_ref[1, at] = demand_ref[:, j, :].astype(f32)
    load_a.wait()

    def home(stage, which, dual):
        base = base_ref[0] - dual * base_ref[1]
        base = jnp.concatenate([base] * (128 // rb), axis=1)
        x = mm(g_ref[...], to_bytes(take_rows(stage))).astype(bf16)
        lanes = CHUNK * rb
        diag = lax.broadcasted_iota(i32, (CHUNK, lanes), 0) == (
            lax.broadcasted_iota(i32, (CHUNK, lanes), 1) // rb
        )
        pulled = []
        for c in range(pairs // CHUNK):
            j, first = divmod(c * CHUNK, per_dev)
            a = a_ref[first:first + CHUNK, j].reshape(lanes, cols)
            bc = base[c * CHUNK:(c + 1) * CHUNK]
            bc = jnp.concatenate([bc] * (lanes // 128), axis=1)
            xc = x[c * CHUNK:(c + 1) * CHUNK]
            xc = jnp.concatenate([xc[:, :cols], xc[:, cols:]], axis=0)
            r = lax.dot_general(xc, a, (((1,), (1,)), ((), ())), preferred_element_type=f32)
            r = (r[:CHUNK] * 256.0 + r[CHUNK:]) * (dual / 32768.0)
            inner = jnp.where(diag, r + bc, 0.0)
            hi = inner.astype(bf16)
            lo = (inner - hi.astype(f32)).astype(bf16)
            g = mm(jnp.concatenate([hi, lo], axis=0), a)
            pulled.append(g[:CHUNK] + g[CHUNK:])
        terms = w_col * (lin_ref[...] + jnp.concatenate(pulled, axis=0))
        peak = jnp.maximum(jnp.max(jnp.abs(terms), axis=1, keepdims=True), 1e-30)
        unit = peak * (1.0 / 32767.0)
        scale_out[which] = jnp.broadcast_to(unit, (pairs, 128)).T[0:1]
        codes = jnp.round(terms / unit) + 32768.0
        codes = jnp.clip(codes, 0.0, 65535.0).astype(i32)
        exchange_start(lambda e: scale_out.at[which], scale_in.at[which], scale_send.at[which], scale_recv.at[which])
        scale_in[which, n - 1] = scale_out[which]
        placed = mm(gt_ref[...], to_bytes(codes))
        placed = (placed[:, :cols] * 256.0 + placed[:, cols:]).astype(i32)
        send_rows(stage + 1, placed)

    def gradient(stage, which):
        wait_all(scale_in.at[which], scale_recv.at[which])
        unit = slot_col(scale_in[which])
        codes = take_rows(stage)
        terms = (codes - 32768).astype(f32) * unit
        return mm_split(e_ref[...], terms)

    home(0, 0, 0.5)
    eq_ref[...] = onehot(local == local_row)
    zone_one = jnp.clip(prior - step * gradient(1, 0), 0.0, high)
    send_rows(2, zone_code(zone_one))
    home(2, 1, 1.0)
    own_t_ref[...] = onehot(local_row == lax.broadcasted_iota(i32, (sb, slots), 0).astype(f32) + 1.0)
    grad = gradient(3, 1) + totals * (zone_one - prior)
    zone_two = jnp.clip(zone_one - step * grad, 0.0, high)
    weighted = w_slot * zone_two
    both = jnp.concatenate([split(weighted), w_wide], axis=1)
    sums = mm(eq_ref[...], both)
    fresh = (prior + (sums[:, :cols] + sums[:, cols:2 * cols])) / (1.0 + sums[:, 2 * cols:])
    delta = jnp.round((zone_two - fresh + 2.0) * 16384.0)
    send_rows(4, jnp.clip(delta, 0.0, 65535.0).astype(i32))
    sums = mm(own_t_ref[...], both)
    fresh_ref[...] = (old_ref[...] + (sums[:, :cols] + sums[:, cols:2 * cols])) / (
        1.0 + sums[:, 2 * cols:]
    )
    out = mm(g_ref[...], to_bytes(take_rows(4)))
    diff = (out[:, :cols] * 256.0 + out[:, cols:]) * (1.0 / 16384.0) - 2.0
    for j in range(touched):
        out_ref[:, j, :] = mult_ref[:, j, :].astype(f32) + diff[j * per_dev:(j + 1) * per_dev]

    wait_all(meta_in, send_sem.at[0])
    for stage in range(5):
        wait_all(rows_in.at[stage], send_sem.at[stage + 1])
    for which in range(2):
        wait_all(scale_in.at[which], scale_send.at[which])


def body(
    constraint, demand, start_duals, unit_cost, multiplier, weight,
    block_index, bundle_of, consensus, capacity_limit,
):
    n = lax.axis_size(("scen", "bund"))
    n_bund = lax.axis_size("bund")
    per_dev, touched, rb, cols = constraint.shape
    pairs = per_dev * touched
    sb = consensus.shape[0] // cols
    capacity = max(2, (2 * per_dev + n - 1) // n)
    rh = -(-capacity * touched // 8) * 8
    half_slots = n * rh
    slots = 2 * half_slots

    vmem = pl.BlockSpec(memory_space=pltpu.VMEM)
    fresh, updated = pl.pallas_call(
        functools.partial(kernel, n, n_bund, rh, sb, rb),
        out_shape=(
            jax.ShapeDtypeStruct((sb, cols), f32),
            jax.ShapeDtypeStruct((per_dev, touched, cols), f32),
        ),
        in_specs=[vmem] * 7 + [pl.BlockSpec(memory_space=pl.ANY)] + [vmem] * 2,
        out_specs=(vmem, vmem),
        scratch_shapes=[
            pltpu.VMEM((1, 3 * pairs), f32),
            pltpu.VMEM((n, 1, 3 * pairs), f32),
            pltpu.VMEM((5, n, rh, cols), i32),
            pltpu.VMEM((5, n, rh, cols), i32),
            pltpu.VMEM((2, 1, pairs), f32),
            pltpu.VMEM((2, n, 1, pairs), f32),
            pltpu.VMEM((slots, slots), bf16),
            pltpu.VMEM((slots, slots), bf16),
            pltpu.VMEM((pairs, slots), bf16),
            pltpu.VMEM((slots, pairs), bf16),
            pltpu.VMEM((slots, sb), bf16),
            pltpu.VMEM((sb, slots), bf16),
            pltpu.VMEM(constraint.shape, bf16),
            pltpu.VMEM((pairs, cols), f32),
            pltpu.VMEM((2, pairs, rb), f32),
            pltpu.SemaphoreType.DMA((6,)),
            pltpu.SemaphoreType.DMA((6,)),
            pltpu.SemaphoreType.DMA((2,)),
            pltpu.SemaphoreType.DMA((2,)),
            pltpu.SemaphoreType.DMA,
        ],
        compiler_params=pltpu.CompilerParams(
            collective_id=0, has_side_effects=True, vmem_limit_bytes=56 * 1024 * 1024
        ),
    )(
        bundle_of.reshape(1, per_dev),
        block_index,
        weight.reshape(1, per_dev),
        unit_cost, multiplier, start_duals, demand, constraint,
        consensus.reshape(sb, cols),
        capacity_limit.reshape(sb, cols),
    )
    return fresh.reshape(-1), updated


def solution(mesh):
    split_all = ("grp", "scen", "bund")
    return jax.shard_map(
        body,
        mesh=mesh,
        in_specs=(
            P(split_all, None, None, None),
            P(split_all, None, None),
            P(split_all, None, None),
            P(split_all, None, None),
            P(split_all, None, None),
            P(split_all),
            P(split_all, None),
            P(split_all),
            P(split_all),
            P(split_all),
        ),
        out_specs=(P(split_all), P(split_all, None, None)),
        check_vma=False,
    )
```

```python
import functools
import jax
import jax.numpy as jnp
from jax import lax
from jax.experimental import pallas as pl
from jax.experimental.pallas import tpu as pltpu
from jax.sharding import PartitionSpec as P

f32 = jnp.float32
bf16 = jnp.bfloat16
i32 = jnp.int32
CHUNK = 16


def split(x):
    hi = x.astype(bf16)
    lo = (x - hi.astype(f32)).astype(bf16)
    return jnp.concatenate([hi, lo], axis=1)


def mm(a, b):
    return jnp.dot(a, b, preferred_element_type=f32)


def mm_split(sel, x):
    out = mm(sel, split(x))
    c = x.shape[1]
    return out[:, :c] + out[:, c:]


def onehot(cond):
    return jnp.where(cond, 1.0, 0.0).astype(bf16)


def to_bytes(q):
    hi = lax.shift_right_logical(q, 8)
    lo = q & 255
    return jnp.concatenate([hi.astype(f32).astype(bf16), lo.astype(f32).astype(bf16)], axis=1)


def pack(q):
    half = q.shape[0] // 2
    return (q[:half] << 16) | q[half:]


def unpack(word):
    return jnp.concatenate([lax.shift_right_logical(word, 16), word & 65535], axis=0)


def kernel(
    n, n_bund, rh, sb, rb,
    bundle_ref, block_ref, weight_ref, unit_ref, mult_ref, dual_ref, demand_ref, a_hbm, old_hbm, high_hbm,
    fresh_ref, out_ref,
    meta_out, meta_in, rows_out, rows_in, scale_out, scale_in,
    e_ref, eq_ref, g_ref, gt_ref, own_ref, own_t_ref, a_ref, lin_ref, base_ref, old_ref, high_ref,
    send_sem, recv_sem, scale_send, scale_recv, load_sem,
):
    me = lax.axis_index("scen") * n_bund + lax.axis_index("bund")
    touched, per_dev = block_ref.shape
    pairs = per_dev * touched
    cols = old_hbm.shape[1]
    half_slots = n * rh
    slots = 2 * half_slots

    bits = n.bit_length() - 1
    mine = [lax.rem(me // (1 << b), 2) for b in range(bits)]

    def device(e):
        d = 0
        for b in range(bits):
            k = lax.rem((e + 1) // (1 << b), 2)
            d = d + (mine[b] + k - 2 * mine[b] * k) * (1 << b)
        return {"scen": d // n_bund, "bund": lax.rem(d, n_bund)}

    barrier = pltpu.get_barrier_semaphore()

    def greet(e, c):
        pl.semaphore_signal(barrier, inc=1, device_id=device(e), device_id_type=pl.DeviceIdType.MESH)
        return c

    lax.fori_loop(0, n - 1, greet, 0, unroll=n <= 16)

    loads = [
        pltpu.make_async_copy(src, dst, load_sem.at[i])
        for i, (src, dst) in enumerate([(old_hbm, old_ref), (high_hbm, high_ref), (a_hbm, a_ref)])
    ]
    for load in loads:
        load.start()

    twice = lambda row: jnp.concatenate([row] * touched, axis=1)
    bun_row = twice(bundle_ref[...].astype(f32))
    w_row = twice(weight_ref[...].astype(f32))
    key_row = jnp.concatenate([block_ref[j:j + 1] for j in range(touched)], axis=1).astype(f32)
    rows = jnp.concatenate([bun_row, w_row, key_row, jnp.zeros((5, pairs), f32)], axis=0)
    rows_t = jnp.concatenate([rows] * (pairs // 8), axis=0).T
    bun_col, w_col, key_col = rows_t[:, 0:1], rows_t[:, 1:2], rows_t[:, 2:3]
    p_row = lax.broadcasted_iota(i32, (1, pairs), 1)
    p_col = lax.broadcasted_iota(i32, (pairs, 1), 0)
    same = bun_col == bun_row
    before = (p_row < per_dev) & (p_row < lax.rem(p_col, per_dev))
    after = (p_col < per_dev) & (p_col < lax.rem(p_row, per_dev))
    cnt_col = jnp.sum(jnp.where(same & before, 1.0, 0.0), axis=1, keepdims=True).astype(i32)
    cnt_row = jnp.sum(jnp.where(same & after, 1.0, 0.0), axis=0, keepdims=True).astype(i32)

    def code(bun, key, cnt, p):
        up = (key.astype(i32) >= sb).astype(i32)
        dest = bun.astype(i32) + up
        dest = jnp.where(dest >= n, dest - n, dest)
        entry = jnp.where(dest == me, n, dest ^ me) - 1
        inner = cnt * touched + p // per_dev
        return dest * (2 * rh) + up * rh + inner, up * half_slots + entry * rh + inner

    full_row, rel_row = code(bun_row, key_row, cnt_row, p_row)
    _, rel_col = code(bun_col, key_col, cnt_col, p_col)
    meta_out[...] = jnp.concatenate([full_row.astype(f32), key_row, w_row], axis=1)
    pl.semaphore_wait(barrier, n - 1)

    def exchange_start(src_of, dst, ssem, rsem):
        def go(k, c):
            e = n - 2 - k
            pltpu.make_async_remote_copy(
                src_ref=src_of(e), dst_ref=dst.at[e], send_sem=ssem, recv_sem=rsem,
                device_id=device(e), device_id_type=pl.DeviceIdType.MESH,
            ).start()
            return c
        lax.fori_loop(0, n - 1, go, 0, unroll=n <= 16)

    def wait_all(buf, sem):
        part = buf.at[pl.ds(0, n - 1)]
        pltpu.make_async_copy(part, part, sem).wait()

    exchange_start(lambda e: meta_out, meta_in, send_sem.at[0], recv_sem.at[0])
    meta_in[n - 1] = meta_out[...]
    g_ref[...] = onehot(rel_col == lax.broadcasted_iota(i32, (pairs, slots), 1))
    gt_ref[...] = onehot(rel_row == lax.broadcasted_iota(i32, (slots, pairs), 0))
    wait_all(meta_in, recv_sem.at[0])

    got = meta_in[...]
    code_in, key_in, w_in = [got[:, :, i * pairs:(i + 1) * pairs] for i in range(3)]

    def slot_mask(h):
        want = me * (2 * rh) + h * rh + lax.broadcasted_iota(i32, (n, rh, pairs), 1)
        return code_in.astype(i32) == want

    masks = [slot_mask(0), slot_mask(1)]

    def slot_col(values):
        return jnp.concatenate(
            [
                jnp.sum(jnp.where(m, values, 0.0), axis=2, keepdims=True).reshape(half_slots, 1)
                for m in masks
            ],
            axis=0,
        )

    keys = slot_col(key_in + 1.0)
    w_slot = slot_col(w_in)
    up_slot = lax.broadcasted_iota(i32, (slots, 1), 0) >= half_slots
    local = jnp.where(up_slot, keys - sb, keys)
    local = jnp.where(keys > 0.0, local, 0.0)
    keys_row = jnp.broadcast_to(keys, (slots, 128)).T[0:1]
    local_row = jnp.broadcast_to(local, (slots, 128)).T[0:1]
    own_ref[...] = onehot(local == lax.broadcasted_iota(i32, (slots, sb), 1).astype(f32) + 1.0)

    def send_rows(stage, codes):
        rows_out[stage] = pack(codes).reshape(n, rh, cols)
        exchange_start(
            lambda e: rows_out.at[stage, e], rows_in.at[stage], send_sem.at[stage + 1], recv_sem.at[stage + 1]
        )
        rows_in[stage, n - 1] = rows_out[stage, n - 1]

    def take_rows(stage):
        wait_all(rows_in.at[stage], recv_sem.at[stage + 1])
        return unpack(rows_in[stage].reshape(half_slots, cols))

    def zone_code(z):
        return jnp.minimum(jnp.round(z * 32768.0), 65535.0).astype(i32)

    loads[0].wait()
    prior = mm_split(own_ref[...], old_ref[...])
    send_rows(0, zone_code(prior))
    loads[1].wait()
    high = mm_split(own_ref[...], high_ref[...])
    e_ref[...] = onehot(keys == keys_row)
    w_wide = jnp.broadcast_to(w_slot, (slots, cols)).astype(bf16)
    totals = mm(e_ref[...], w_wide)
    step = 0.5 / (1.0 + totals)

    for j in range(touched):
        at = slice(j * per_dev, (j + 1) * per_dev)
        lin_ref[at] = unit_ref[:, j, :].astype(f32) + mult_ref[:, j, :].astype(f32)
        base_ref[0, at] = dual_ref[:, j, :].astype(f32)
        base_ref[1, at] = demand_ref[:, j, :].astype(f32)
    loads[2].wait()

    def home(stage, which, dual):
        base = base_ref[0] - dual * base_ref[1]
        base = jnp.concatenate([base] * (128 // rb), axis=1)
        x = mm(g_ref[...], to_bytes(take_rows(stage))).astype(bf16)
        lanes = CHUNK * rb
        diag = lax.broadcasted_iota(i32, (CHUNK, lanes), 0) == (
            lax.broadcasted_iota(i32, (CHUNK, lanes), 1) // rb
        )
        pulled = []
        for c in range(pairs // CHUNK):
            j, first = divmod(c * CHUNK, per_dev)
            a = a_ref[first:first + CHUNK, j].reshape(lanes, cols)
            bc = base[c * CHUNK:(c + 1) * CHUNK]
            bc = jnp.concatenate([bc] * (lanes // 128), axis=1)
            xc = x[c * CHUNK:(c + 1) * CHUNK]
            xc = jnp.concatenate([xc[:, :cols], xc[:, cols:]], axis=0)
            r = lax.dot_general(xc, a, (((1,), (1,)), ((), ())), preferred_element_type=f32)
            r = (r[:CHUNK] * 256.0 + r[CHUNK:]) * (dual / 32768.0)
            inner = jnp.where(diag, r + bc, 0.0)
            hi = inner.astype(bf16)
            lo = (inner - hi.astype(f32)).astype(bf16)
            g = mm(jnp.concatenate([hi, lo], axis=0), a)
            pulled.append(g[:CHUNK] + g[CHUNK:])
        terms = w_col * (lin_ref[...] + jnp.concatenate(pulled, axis=0))
        peak = jnp.maximum(jnp.max(jnp.abs(terms), axis=1, keepdims=True), 1e-30)
        unit = peak * (1.0 / 32767.0)
        scale_out[which] = jnp.broadcast_to(unit, (pairs, 128)).T[0:1]
        codes = jnp.round(terms / unit) + 32768.0
        codes = jnp.clip(codes, 0.0, 65535.0).astype(i32)
        exchange_start(lambda e: scale_out.at[which], scale_in.at[which], scale_send.at[which], scale_recv.at[which])
        scale_in[which, n - 1] = scale_out[which]
        placed = mm(gt_ref[...], to_bytes(codes))
        placed = (placed[:, :cols] * 256.0 + placed[:, cols:]).astype(i32)
        send_rows(stage + 1, placed)

    def gradient(stage, which):
        wait_all(scale_in.at[which], scale_recv.at[which])
        unit = slot_col(scale_in[which])
        codes = take_rows(stage)
        terms = (codes - 32768).astype(f32) * unit
        return mm_split(e_ref[...], terms)

    home(0, 0, 0.5)
    eq_ref[...] = onehot(local == local_row)
    zone_one = jnp.clip(prior - step * gradient(1, 0), 0.0, high)
    send_rows(2, zone_code(zone_one))
    home(2, 1, 1.0)
    own_t_ref[...] = onehot(local_row == lax.broadcasted_iota(i32, (sb, slots), 0).astype(f32) + 1.0)
    grad = gradient(3, 1) + totals * (zone_one - prior)
    zone_two = jnp.clip(zone_one - step * grad, 0.0, high)
    weighted = w_slot * zone_two
    both = jnp.concatenate([split(weighted), w_wide], axis=1)
    sums = mm(eq_ref[...], both)
    fresh = (prior + (sums[:, :cols] + sums[:, cols:2 * cols])) / (1.0 + sums[:, 2 * cols:])
    delta = jnp.round((zone_two - fresh + 2.0) * 16384.0)
    send_rows(4, jnp.clip(delta, 0.0, 65535.0).astype(i32))
    sums = mm(own_t_ref[...], both)
    fresh_ref[...] = (old_ref[...] + (sums[:, :cols] + sums[:, cols:2 * cols])) / (
        1.0 + sums[:, 2 * cols:]
    )
    out = mm(g_ref[...], to_bytes(take_rows(4)))
    diff = (out[:, :cols] * 256.0 + out[:, cols:]) * (1.0 / 16384.0) - 2.0
    for j in range(touched):
        out_ref[:, j, :] = mult_ref[:, j, :].astype(f32) + diff[j * per_dev:(j + 1) * per_dev]

    wait_all(meta_in, send_sem.at[0])
    for stage in range(5):
        wait_all(rows_in.at[stage], send_sem.at[stage + 1])
    for which in range(2):
        wait_all(scale_in.at[which], scale_send.at[which])


def hand_on(fresh_in, updated_in, fresh_ref, updated_ref, sem):
    copies = [
        pltpu.make_async_copy(fresh_in, fresh_ref, sem.at[0]),
        pltpu.make_async_copy(updated_in, updated_ref, sem.at[1]),
    ]
    for copy in copies:
        copy.start()
    for copy in copies:
        copy.wait()


def body(
    constraint, demand, start_duals, unit_cost, multiplier, weight,
    block_index, bundle_of, consensus, capacity_limit,
):
    n = lax.axis_size(("scen", "bund"))
    n_bund = lax.axis_size("bund")
    per_dev, touched, rb, cols = constraint.shape
    pairs = per_dev * touched
    sb = consensus.shape[0] // cols
    capacity = max(2, (2 * per_dev + n - 1) // n)
    rh = -(-capacity * touched // 8) * 8
    half_slots = n * rh
    slots = 2 * half_slots

    vmem = pl.BlockSpec(memory_space=pltpu.VMEM)
    anywhere = pl.BlockSpec(memory_space=pl.ANY)
    fresh, updated = pl.pallas_call(
        functools.partial(kernel, n, n_bund, rh, sb, rb),
        out_shape=(
            jax.ShapeDtypeStruct((sb, cols), f32),
            jax.ShapeDtypeStruct((per_dev, touched, cols), f32),
        ),
        in_specs=[vmem] * 7 + [anywhere] * 3,
        out_specs=(vmem, vmem),
        scratch_shapes=[
            pltpu.VMEM((1, 3 * pairs), f32),
            pltpu.VMEM((n, 1, 3 * pairs), f32),
            pltpu.VMEM((5, n, rh, cols), i32),
            pltpu.VMEM((5, n, rh, cols), i32),
            pltpu.VMEM((2, 1, pairs), f32),
            pltpu.VMEM((2, n, 1, pairs), f32),
            pltpu.VMEM((slots, slots), bf16),
            pltpu.VMEM((slots, slots), bf16),
            pltpu.VMEM((pairs, slots), bf16),
            pltpu.VMEM((slots, pairs), bf16),
            pltpu.VMEM((slots, sb), bf16),
            pltpu.VMEM((sb, slots), bf16),
            pltpu.VMEM(constraint.shape, bf16),
            pltpu.VMEM((pairs, cols), f32),
            pltpu.VMEM((2, pairs, rb), f32),
            pltpu.VMEM((sb, cols), f32),
            pltpu.VMEM((sb, cols), f32),
            pltpu.SemaphoreType.DMA((6,)),
            pltpu.SemaphoreType.DMA((6,)),
            pltpu.SemaphoreType.DMA((2,)),
            pltpu.SemaphoreType.DMA((2,)),
            pltpu.SemaphoreType.DMA((3,)),
        ],
        compiler_params=pltpu.CompilerParams(
            collective_id=0, has_side_effects=True, vmem_limit_bytes=56 * 1024 * 1024
        ),
    )(
        bundle_of.reshape(1, per_dev),
        block_index.T,
        weight.reshape(1, per_dev),
        unit_cost, multiplier, start_duals, demand, constraint,
        consensus.reshape(sb, cols),
        capacity_limit.reshape(sb, cols),
    )
    fresh, updated = pl.pallas_call(
        hand_on,
        out_shape=(
            jax.ShapeDtypeStruct(fresh.shape, f32),
            jax.ShapeDtypeStruct(updated.shape, f32),
        ),
        in_specs=[vmem] * 2,
        out_specs=(anywhere, anywhere),
        scratch_shapes=[pltpu.SemaphoreType.DMA((2,))],
    )(fresh, updated)
    return fresh.reshape(-1), updated


def solution(mesh):
    split_all = ("grp", "scen", "bund")
    return jax.shard_map(
        body,
        mesh=mesh,
        in_specs=(
            P(split_all, None, None, None),
            P(split_all, None, None),
            P(split_all, None, None),
            P(split_all, None, None),
            P(split_all, None, None),
            P(split_all),
            P(split_all, None),
            P(split_all),
            P(split_all),
            P(split_all),
        ),
        out_specs=(P(split_all), P(split_all, None, None)),
        check_vma=False,
    )
```

```python
import functools
import jax
import jax.numpy as jnp
from jax import lax
from jax.experimental import pallas as pl
from jax.experimental.pallas import tpu as pltpu
from jax.sharding import PartitionSpec as P

f32 = jnp.float32
bf16 = jnp.bfloat16
i32 = jnp.int32
CHUNK = 16


def split(x):
    hi = x.astype(bf16)
    lo = (x - hi.astype(f32)).astype(bf16)
    return jnp.concatenate([hi, lo], axis=1)


def mm(a, b):
    return jnp.dot(a, b, preferred_element_type=f32)


def mm_split(sel, x):
    out = mm(sel, split(x))
    c = x.shape[1]
    return out[:, :c] + out[:, c:]


def onehot(cond):
    return jnp.where(cond, 1.0, 0.0).astype(bf16)


def to_bytes(q):
    hi = lax.shift_right_logical(q, 8)
    lo = q & 255
    return jnp.concatenate([hi.astype(f32).astype(bf16), lo.astype(f32).astype(bf16)], axis=1)


def pack(q):
    half = q.shape[0] // 2
    return (q[:half] << 16) | q[half:]


def unpack(word):
    return jnp.concatenate([lax.shift_right_logical(word, 16), word & 65535], axis=0)


def kernel(
    n, n_bund, rh, sb, rb,
    bundle_ref, block_ref, weight_ref, unit_ref, mult_ref, dual_ref, demand_ref, a_hbm, old_hbm, high_hbm,
    fresh_ref, out_ref,
    meta_out, meta_in, rows_out, rows_in, scale_out, scale_in,
    e_ref, eq_ref, g_ref, gt_ref, own_ref, own_t_ref, a_ref, wide_ref, wide_t_ref, lin_ref, base_ref, old_ref, high_ref,
    send_sem, recv_sem, scale_send, scale_recv, load_sem,
):
    me = lax.axis_index("scen") * n_bund + lax.axis_index("bund")
    touched, per_dev = block_ref.shape
    pairs = per_dev * touched
    cols = old_hbm.shape[1]
    half_slots = n * rh
    slots = 2 * half_slots
    near = n // 2
    group_slots = slots // 2
    groups = [slice(0, group_slots), slice(group_slots, slots)]

    bits = n.bit_length() - 1
    mine = [lax.rem(me // (1 << b), 2) for b in range(bits)]

    def device(x):
        d = 0
        for b in range(bits):
            k = lax.rem(x // (1 << b), 2)
            d = d + (mine[b] + k - 2 * mine[b] * k) * (1 << b)
        return {"scen": d // n_bund, "bund": lax.rem(d, n_bund)}

    barrier = pltpu.get_barrier_semaphore()

    def greet(e, c):
        pl.semaphore_signal(barrier, inc=1, device_id=device(e), device_id_type=pl.DeviceIdType.MESH)
        return c

    lax.fori_loop(1, n, greet, 0, unroll=n <= 16)

    loads = [
        pltpu.make_async_copy(src, dst, load_sem.at[i])
        for i, (src, dst) in enumerate([(old_hbm, old_ref), (high_hbm, high_ref), (a_hbm, a_ref)])
    ]
    for load in loads:
        load.start()

    twice = lambda row: jnp.concatenate([row] * touched, axis=1)
    bun_row = twice(bundle_ref[...].astype(f32))
    w_row = twice(weight_ref[...].astype(f32))
    key_row = jnp.concatenate([block_ref[j:j + 1] for j in range(touched)], axis=1).astype(f32)
    rows = jnp.concatenate([bun_row, w_row, key_row, jnp.zeros((5, pairs), f32)], axis=0)
    rows_t = jnp.concatenate([rows] * (pairs // 8), axis=0).T
    bun_col, w_col, key_col = rows_t[:, 0:1], rows_t[:, 1:2], rows_t[:, 2:3]
    p_row = lax.broadcasted_iota(i32, (1, pairs), 1)
    p_col = lax.broadcasted_iota(i32, (pairs, 1), 0)
    same = bun_col == bun_row
    before = (p_row < per_dev) & (p_row < lax.rem(p_col, per_dev))
    after = (p_col < per_dev) & (p_col < lax.rem(p_row, per_dev))
    cnt_col = jnp.sum(jnp.where(same & before, 1.0, 0.0), axis=1, keepdims=True).astype(i32)
    cnt_row = jnp.sum(jnp.where(same & after, 1.0, 0.0), axis=0, keepdims=True).astype(i32)

    def code(bun, key, cnt, p):
        up = (key.astype(i32) >= sb).astype(i32)
        dest = bun.astype(i32) + up
        dest = jnp.where(dest >= n, dest - n, dest)
        entry = dest ^ me
        far = (entry >= near).astype(i32)
        inner = cnt * touched + p // per_dev
        slot = far * group_slots + up * (near * rh) + (entry - far * near) * rh + inner
        return dest * (2 * rh) + up * rh + inner, slot

    full_row, rel_row = code(bun_row, key_row, cnt_row, p_row)
    _, rel_col = code(bun_col, key_col, cnt_col, p_col)
    meta_out[...] = jnp.concatenate([full_row.astype(f32), key_row, w_row], axis=1)
    pl.semaphore_wait(barrier, n - 1)

    def send_group(g, messages):
        first, last = (1, near) if g == 0 else (near, n)

        def go(k, c):
            x = first + last - 1 - k
            for src_of, dst, ssem, rsem in messages:
                pltpu.make_async_remote_copy(
                    src_ref=src_of(x), dst_ref=dst.at[x], send_sem=ssem, recv_sem=rsem.at[g],
                    device_id=device(x), device_id_type=pl.DeviceIdType.MESH,
                ).start()
            return c
        lax.fori_loop(first, last, go, 0, unroll=n <= 16)

    def wait_part(buf, first, last, sem):
        part = buf.at[pl.ds(first, last - first)]
        pltpu.make_async_copy(part, part, sem).wait()

    def wait_group(g, buf, sem):
        first, last = (1, near) if g == 0 else (near, n)
        wait_part(buf, first, last, sem.at[g])

    def wait_sent(buf, sem):
        wait_part(buf, 1, n, sem)

    for g in (1, 0):
        send_group(g, [(lambda x: meta_out, meta_in, send_sem.at[0], recv_sem.at[0])])
    meta_in[0] = meta_out[...]
    g_ref[...] = onehot(rel_col == lax.broadcasted_iota(i32, (pairs, slots), 1))
    gt_ref[...] = onehot(rel_row == lax.broadcasted_iota(i32, (slots, pairs), 0))

    lanes = CHUNK * rb
    loads[2].wait()
    for c in range(pairs // (2 * CHUNK)):
        j, first = divmod(2 * c * CHUNK, per_dev)
        a = [a_ref[f:f + CHUNK, j].reshape(lanes, cols) for f in (first, first + CHUNK)]
        wide_ref[c] = jnp.concatenate(a, axis=1)
        wide_t_ref[c] = jnp.concatenate([m.T for m in a], axis=0)

    masks, key_parts, w_parts = [], [], []

    def slot_col(g, values):
        return jnp.concatenate(
            [
                jnp.sum(jnp.where(m, values, 0.0), axis=2, keepdims=True).reshape(near * rh, 1)
                for m in masks[g]
            ],
            axis=0,
        )

    for g in (0, 1):
        wait_group(g, meta_in, recv_sem.at[0])
        got = meta_in[g * near:(g + 1) * near]
        code_in, key_in, w_in = [got[:, :, i * pairs:(i + 1) * pairs] for i in range(3)]
        want = me * (2 * rh) + lax.broadcasted_iota(i32, (near, rh, pairs), 1)
        masks.append([code_in.astype(i32) == want, code_in.astype(i32) == want + rh])
        key_parts.append(slot_col(g, key_in + 1.0))
        w_parts.append(slot_col(g, w_in))
    keys = jnp.concatenate(key_parts, axis=0)
    up_slot = lax.rem(lax.broadcasted_iota(i32, (slots, 1), 0), group_slots) >= near * rh
    local = jnp.where(up_slot, keys - sb, keys)
    local = jnp.where(keys > 0.0, local, 0.0)

    def send_rows(stage, g, codes, more=()):
        rows_out[stage, g * near:(g + 1) * near] = pack(codes).reshape(near, rh, cols)
        rows = (lambda x: rows_out.at[stage, x], rows_in.at[stage], send_sem.at[stage + 1], recv_sem.at[stage + 1])
        send_group(g, [*more, rows])
        if g == 0:
            rows_in[stage, 0] = rows_out[stage, 0]

    def take_rows(stage, g):
        wait_group(g, rows_in.at[stage], recv_sem.at[stage + 1])
        return unpack(rows_in[stage, g * near:(g + 1) * near].reshape(near * rh, cols))

    def zone_code(z):
        return jnp.minimum(jnp.round(z * 32768.0), 65535.0).astype(i32)

    prior = [None, None]
    loads[0].wait()
    old_parts = split(old_ref[...])
    for g in (1, 0):
        own = onehot(local[groups[g]] == lax.broadcasted_iota(i32, (group_slots, sb), 1).astype(f32) + 1.0)
        own_ref[groups[g]] = own
        picked = mm(own, old_parts)
        prior[g] = picked[:, :cols] + picked[:, cols:]
        send_rows(0, g, zone_code(prior[g]))
    keys_row = jnp.broadcast_to(keys, (slots, 128)).T[0:1]
    local_row = jnp.broadcast_to(local, (slots, 128)).T[0:1]
    loads[1].wait()
    high = mm_split(own_ref[...], high_ref[...])
    high = [high[g] for g in groups]
    e_ref[...] = onehot(keys == keys_row)
    w_wide = [jnp.broadcast_to(w, (group_slots, cols)).astype(bf16) for w in w_parts]
    totals = mm(e_ref[...], jnp.concatenate(w_wide, axis=0))
    totals = [totals[g] for g in groups]
    step = [0.5 / (1.0 + t) for t in totals]
    for j in range(touched):
        at = slice(j * per_dev, (j + 1) * per_dev)
        lin_ref[at] = unit_ref[:, j, :].astype(f32) + mult_ref[:, j, :].astype(f32)
        base_ref[0, at] = dual_ref[:, j, :].astype(f32)
        base_ref[1, at] = demand_ref[:, j, :].astype(f32)

    def pick(stage):
        near_rows = mm(g_ref[:, groups[0]], to_bytes(take_rows(stage, 0)))
        return near_rows + mm(g_ref[:, groups[1]], to_bytes(take_rows(stage, 1)))

    def home(stage, which, dual):
        base = base_ref[0] - dual * base_ref[1]
        base = jnp.concatenate([base] * (128 // rb), axis=1)
        x = pick(stage)
        both_rows = 2 * CHUNK
        diag = lax.rem(lax.broadcasted_iota(i32, (both_rows, lanes), 0), CHUNK) == (
            lax.broadcasted_iota(i32, (both_rows, lanes), 1) // rb
        )
        first_chunk = lax.broadcasted_iota(i32, (both_rows, cols), 0) < CHUNK
        pulled = []
        for c in range(pairs // both_rows):
            at = slice(c * both_rows, (c + 1) * both_rows)
            bc = jnp.concatenate([base[at]] * (lanes // 128), axis=1)
            xc = jnp.concatenate(
                [
                    jnp.concatenate([jnp.where(first_chunk, v, 0.0), jnp.where(first_chunk, 0.0, v)], axis=1)
                    for v in (x[at, :cols], x[at, cols:])
                ],
                axis=0,
            ).astype(bf16)
            r = mm(xc, wide_t_ref[c])
            r = (r[:both_rows] * 256.0 + r[both_rows:]) * (dual / 32768.0)
            inner = jnp.where(diag, r + bc, 0.0)
            hi = inner.astype(bf16)
            lo = (inner - hi.astype(f32)).astype(bf16)
            g = mm(jnp.concatenate([hi, lo], axis=0), wide_ref[c])
            g = g[:both_rows] + g[both_rows:]
            pulled.append(jnp.where(first_chunk, g[:, :cols], g[:, cols:]))
        terms = w_col * (lin_ref[...] + jnp.concatenate(pulled, axis=0))
        peak = jnp.maximum(jnp.max(jnp.abs(terms), axis=1, keepdims=True), 1e-30)
        unit = peak * (1.0 / 32767.0)
        scale_out[which] = jnp.broadcast_to(unit, (pairs, 128)).T[0:1]
        codes = jnp.round(terms / unit) + 32768.0
        codes = jnp.clip(codes, 0.0, 65535.0).astype(i32)
        scale_in[which, 0] = scale_out[which]
        scale = (lambda x: scale_out.at[which], scale_in.at[which], scale_send.at[which], scale_recv.at[which])
        codes = to_bytes(codes)
        for g in (1, 0):
            placed = mm(gt_ref[groups[g]], codes)
            placed = (placed[:, :cols] * 256.0 + placed[:, cols:]).astype(i32)
            send_rows(stage + 1, g, placed, [scale])

    def terms_in(stage, which, g):
        wait_group(g, scale_in.at[which], scale_recv.at[which])
        unit = slot_col(g, scale_in[which, g * near:(g + 1) * near])
        return (take_rows(stage, g) - 32768).astype(f32) * unit

    def gradient(stage, which):
        from_near = mm_split(e_ref[:, groups[0]], terms_in(stage, which, 0))
        far = split(terms_in(stage, which, 1))

        def total(g):
            out = mm(e_ref[groups[g], groups[1]], far)
            return from_near[groups[g]] + (out[:, :cols] + out[:, cols:])
        return total

    home(0, 0, 0.5)
    eq_ref[...] = onehot(local == local_row)
    grad = gradient(1, 0)
    zone_one = [None, None]
    for g in (1, 0):
        zone_one[g] = jnp.clip(prior[g] - step[g] * grad(g), 0.0, high[g])
        send_rows(2, g, zone_code(zone_one[g]))
    home(2, 1, 1.0)
    own_t_ref[...] = onehot(local_row == lax.broadcasted_iota(i32, (sb, slots), 0).astype(f32) + 1.0)
    grad = gradient(3, 1)
    zone_two, both = [None, None], [None, None]
    for g in (1, 0):
        pull = grad(g) + totals[g] * (zone_one[g] - prior[g])
        zone_two[g] = jnp.clip(zone_one[g] - step[g] * pull, 0.0, high[g])
        both[g] = jnp.concatenate([split(w_parts[g] * zone_two[g]), w_wide[g]], axis=1)
    both = jnp.concatenate(both, axis=0)
    for g in (1, 0):
        sums = mm(eq_ref[groups[g]], both)
        fresh = (prior[g] + (sums[:, :cols] + sums[:, cols:2 * cols])) / (1.0 + sums[:, 2 * cols:])
        delta = jnp.round((zone_two[g] - fresh + 2.0) * 16384.0)
        send_rows(4, g, jnp.clip(delta, 0.0, 65535.0).astype(i32))
    sums = mm(own_t_ref[...], both)
    fresh_ref[...] = (old_ref[...] + (sums[:, :cols] + sums[:, cols:2 * cols])) / (
        1.0 + sums[:, 2 * cols:]
    )
    out = pick(4)
    diff = (out[:, :cols] * 256.0 + out[:, cols:]) * (1.0 / 16384.0) - 2.0
    for j in range(touched):
        out_ref[:, j, :] = mult_ref[:, j, :].astype(f32) + diff[j * per_dev:(j + 1) * per_dev]

    wait_sent(meta_in, send_sem.at[0])
    for stage in range(5):
        wait_sent(rows_in.at[stage], send_sem.at[stage + 1])
    for which in range(2):
        wait_sent(scale_in.at[which], scale_send.at[which])


def hand_on(fresh_in, updated_in, fresh_ref, updated_ref, sem):
    copies = [
        pltpu.make_async_copy(fresh_in, fresh_ref, sem.at[0]),
        pltpu.make_async_copy(updated_in, updated_ref, sem.at[1]),
    ]
    for copy in copies:
        copy.start()
    for copy in copies:
        copy.wait()


def body(
    constraint, demand, start_duals, unit_cost, multiplier, weight,
    block_index, bundle_of, consensus, capacity_limit,
):
    n = lax.axis_size(("scen", "bund"))
    n_bund = lax.axis_size("bund")
    per_dev, touched, rb, cols = constraint.shape
    pairs = per_dev * touched
    sb = consensus.shape[0] // cols
    capacity = max(2, (2 * per_dev + n - 1) // n)
    rh = -(-capacity * touched // 8) * 8
    half_slots = n * rh
    slots = 2 * half_slots

    vmem = pl.BlockSpec(memory_space=pltpu.VMEM)
    anywhere = pl.BlockSpec(memory_space=pl.ANY)
    fresh, updated = pl.pallas_call(
        functools.partial(kernel, n, n_bund, rh, sb, rb),
        out_shape=(
            jax.ShapeDtypeStruct((sb, cols), f32),
            jax.ShapeDtypeStruct((per_dev, touched, cols), f32),
        ),
        in_specs=[vmem] * 7 + [anywhere] * 3,
        out_specs=(vmem, vmem),
        scratch_shapes=[
            pltpu.VMEM((1, 3 * pairs), f32),
            pltpu.VMEM((n, 1, 3 * pairs), f32),
            pltpu.VMEM((5, n, rh, cols), i32),
            pltpu.VMEM((5, n, rh, cols), i32),
            pltpu.VMEM((2, 1, pairs), f32),
            pltpu.VMEM((2, n, 1, pairs), f32),
            pltpu.VMEM((slots, slots), bf16),
            pltpu.VMEM((slots, slots), bf16),
            pltpu.VMEM((pairs, slots), bf16),
            pltpu.VMEM((slots, pairs), bf16),
            pltpu.VMEM((slots, sb), bf16),
            pltpu.VMEM((sb, slots), bf16),
            pltpu.VMEM(constraint.shape, bf16),
            pltpu.VMEM((pairs // (2 * CHUNK), CHUNK * rb, 2 * cols), bf16),
            pltpu.VMEM((pairs // (2 * CHUNK), 2 * cols, CHUNK * rb), bf16),
            pltpu.VMEM((pairs, cols), f32),
            pltpu.VMEM((2, pairs, rb), f32),
            pltpu.VMEM((sb, cols), f32),
            pltpu.VMEM((sb, cols), f32),
            pltpu.SemaphoreType.DMA((6,)),
            pltpu.SemaphoreType.DMA((6, 2)),
            pltpu.SemaphoreType.DMA((2,)),
            pltpu.SemaphoreType.DMA((2, 2)),
            pltpu.SemaphoreType.DMA((3,)),
        ],
        compiler_params=pltpu.CompilerParams(
            collective_id=0, has_side_effects=True, vmem_limit_bytes=56 * 1024 * 1024
        ),
    )(
        bundle_of.reshape(1, per_dev),
        block_index.T,
        weight.reshape(1, per_dev),
        unit_cost, multiplier, start_duals, demand, constraint,
        consensus.reshape(sb, cols),
        capacity_limit.reshape(sb, cols),
    )
    fresh, updated = pl.pallas_call(
        hand_on,
        out_shape=(
            jax.ShapeDtypeStruct(fresh.shape, f32),
            jax.ShapeDtypeStruct(updated.shape, f32),
        ),
        in_specs=[vmem] * 2,
        out_specs=(anywhere, anywhere),
        scratch_shapes=[pltpu.SemaphoreType.DMA((2,))],
    )(fresh, updated)
    return fresh.reshape(-1), updated


def solution(mesh):
    split_all = ("grp", "scen", "bund")
    return jax.shard_map(
        body,
        mesh=mesh,
        in_specs=(
            P(split_all, None, None, None),
            P(split_all, None, None),
            P(split_all, None, None),
            P(split_all, None, None),
            P(split_all, None, None),
            P(split_all),
            P(split_all, None),
            P(split_all),
            P(split_all),
            P(split_all),
        ),
        out_specs=(P(split_all), P(split_all, None, None)),
        check_vma=False,
    )
```
